256 devices in a mesh: section: 2 (over y_lo), dp: 8 (over z), tensor: 16 (over x, y_hi, core).
Axes of the slice: x: 4, y: 4 (y_hi: 2, y_lo: 2; y = y_hi * 2 + y_lo), z: 8, core: 2. Of those that a mesh axis runs over, the one named last changes fastest.
Arguments:
- inputs: bfloat16 [2, 512, 6144], P(None, 'dp'), may hold values from -6 to 6
- cotangent: bfloat16 [2, 512, 6144], P(None, 'dp'), may hold values from -6 to 6
- gate_weight: bfloat16 [2, 6144, 6144], P('section', 'tensor', 'dp'), may hold values from -0.078125 to 0.078125
- up_weight: bfloat16 [2, 6144, 6144], P('section', 'tensor', 'dp'), may hold values from -0.078125 to 0.078125
- down_weight: bfloat16 [2, 6144, 6144], P('section', 'tensor', 'dp'), may hold values from -0.078125 to 0.078125
Outputs:
- section_out: bfloat16 [2, 2, 512, 6144], P('section', None, ('dp', 'tensor'))
- section_grad: bfloat16 [2, 2, 512, 6144], P('section', None, ('dp', 'tensor'))
- grad_gate: bfloat16 [2, 6144, 6144], P('section', 'tensor', 'dp')
- grad_up: bfloat16 [2, 6144, 6144], P('section', 'tensor', 'dp')
- grad_down: bfloat16 [2, 6144, 6144], P('section', 'tensor', 'dp')
The draws below stay inside these ranges and needn't reach their ends.
All inputs are finite; a program needn't handle non-finite values.
Results may differ from the reference program's by a relative error of at most 0.03.
Values may be sent and summed in bfloat16 or wider, within the bound.
A program may use at most 128 MiB of HBM per device.

```python
import math
import jax
import jax.numpy as jnp
from jax import lax

D = 6144
FF_T = 384
TOK_DEV = 64
MICRO = 2
FF = 6144
TOKENS = 512
N_DP = 8
N_TENSOR = 16


def block_levels(stream_key, dims, cuts, least, high):
    gain, own = 1.0, jax.random.fold_in(stream_key, 6)
    for axis_at, shards_of in cuts:
        heights = jnp.exp(jax.random.uniform(jax.random.fold_in(own, axis_at), (shards_of,), jnp.float32, least / len(cuts), high / len(cuts)))
        gain = gain * jnp.repeat(heights, dims[axis_at] // shards_of).reshape([-1 if axis == axis_at else 1 for axis in range(len(dims))])
    return gain


def noise(own_key, dims, scale, limit, shards=(), held_as=jnp.bfloat16):
    factor_of = block_levels(own_key, dims, shards, -0.22, 0.18) if shards else 1.0
    result = jax.random.normal(own_key, dims, jnp.float32) * scale * factor_of
    return jnp.minimum(jnp.maximum(result, -limit), limit).astype(held_as)


def setup_inputs(seed: int = 0) -> dict:
    splits = jax.random.split(jax.random.key(seed), 6)
    inputs = noise(splits[0], (MICRO, TOKENS, D), 1.0, 6.0, ((1, 8),))
    cotangent = noise(splits[1], (MICRO, TOKENS, D), 1.0, 6.0, ((1, 8),))
    gate_weight = noise(splits[2], (2, FF, D), D ** -0.5, 0.078125, ((0, 2), (1, 16), (2, 8)))
    up_weight = noise(splits[3], (2, FF, D), D ** -0.5, 0.078125, ((0, 2), (1, 16), (2, 8)))
    down_weight = noise(splits[4], (2, FF, D), FF ** -0.5, 0.078125, ((0, 2), (1, 16), (2, 8)))
    return dict(inputs=inputs, cotangent=cotangent, gate_weight=gate_weight, up_weight=up_weight, down_weight=down_weight)


def norm_parts(x):
    xf = x.astype(jnp.float32)
    r = lax.rsqrt(lax.optimization_barrier(jnp.mean(xf * xf, axis=-1, keepdims=True)) + 1e-05)
    return (xf, r, (xf * r).astype(jnp.bfloat16))

def forward_block(x, wg, wu, wd):
    xf, r, n = norm_parts(x)
    a = jnp.dot(n, wg.T, preferred_element_type=jnp.float32)
    b = jnp.dot(n, wu.T, preferred_element_type=jnp.float32)
    sig = jax.nn.sigmoid(a)
    h = (a * sig * b).astype(jnp.bfloat16)
    total = jnp.zeros(xf.shape, jnp.float32)
    for group in range(N_TENSOR):
        lo = group * FF_T
        part = jnp.dot(h[:, lo:lo + FF_T], wd[lo:lo + FF_T], preferred_element_type=jnp.float32).astype(jnp.bfloat16)
        total = total + lax.optimization_barrier(part).astype(jnp.float32)
    y = (xf + total).astype(jnp.bfloat16)
    return (y, (xf, r, n, a, b, h))

def backward_block(g, saved, wg, wu, wd):
    xf, r, n, a, b, h = saved
    dh = jnp.dot(g, wd.T, preferred_element_type=jnp.float32)
    sig = jax.nn.sigmoid(a)
    da = (dh * b * sig * (1.0 + a * (1.0 - sig))).astype(jnp.bfloat16)
    db = (dh * a * sig).astype(jnp.bfloat16)
    dn = jnp.zeros(xf.shape, jnp.float32)
    for group in range(N_TENSOR):
        lo = group * FF_T
        part = jnp.dot(da[:, lo:lo + FF_T], wg[lo:lo + FF_T], preferred_element_type=jnp.float32)
        part = part + jnp.dot(db[:, lo:lo + FF_T], wu[lo:lo + FF_T], preferred_element_type=jnp.float32)
        dn = dn + lax.optimization_barrier(part.astype(jnp.bfloat16)).astype(jnp.float32)
    mixed = lax.optimization_barrier(jnp.mean(dn * xf, axis=-1, keepdims=True))
    dx = (g.astype(jnp.float32) + r * (dn - xf * r * r * mixed)).astype(jnp.bfloat16)
    return (dx, da, db)

def group_grad(left, right, scale):
    left = jnp.stack(left).reshape(MICRO, N_DP, TOK_DEV, -1)
    right = jnp.stack(right).reshape(MICRO, N_DP, TOK_DEV, -1)
    total = jnp.zeros((left.shape[-1], right.shape[-1]), jnp.float32)
    for group in range(N_DP):
        lhs = left[:, group].reshape(MICRO * TOK_DEV, -1)
        rhs = right[:, group].reshape(MICRO * TOK_DEV, -1)
        part = (jnp.dot(lhs.T, rhs, preferred_element_type=jnp.float32) * scale).astype(jnp.bfloat16)
        total = total + lax.optimization_barrier(part).astype(jnp.float32)
    return total.astype(jnp.bfloat16)

def reference(inputs, cotangent, gate_weight, up_weight, down_weight):
    weights = [(gate_weight[s], up_weight[s], down_weight[s]) for s in range(2)]
    first_out, second_out, first_saved, second_saved = ([], [], [], [])
    for micro_index in range(MICRO):
        y1, saved1 = forward_block(inputs[micro_index], *weights[0])
        y2, saved2 = forward_block(y1, *weights[1])
        first_out.append(y1)
        second_out.append(y2)
        first_saved.append(saved1)
        second_saved.append(saved2)
    first_grad, second_grad = ([], [])
    first_pieces, second_pieces = ([], [])
    for micro_index in range(MICRO):
        dy1, da2, db2 = backward_block(cotangent[micro_index], second_saved[micro_index], *weights[1])
        dinput, da1, db1 = backward_block(dy1, first_saved[micro_index], *weights[0])
        second_grad.append(dy1)
        first_grad.append(dinput)
        second_pieces.append((cotangent[micro_index], da2, db2))
        first_pieces.append((dy1, da1, db1))
    scale = 1.0 / math.sqrt(MICRO * TOKENS)
    grads = []
    for saved_list, pieces in ((first_saved, first_pieces), (second_saved, second_pieces)):
        hs = [item[5] for item in saved_list]
        ns = [item[2] for item in saved_list]
        gs = [item[0] for item in pieces]
        das = [item[1] for item in pieces]
        dbs = [item[2] for item in pieces]
        grads.append((group_grad(das, ns, scale), group_grad(dbs, ns, scale), group_grad(hs, gs, scale)))
    section_out = jnp.stack([jnp.stack(first_out), jnp.stack(second_out)])
    section_grad = jnp.stack([jnp.stack(first_grad), jnp.stack(second_grad)])
    grad_gate = jnp.stack([grads[0][0], grads[1][0]])
    grad_up = jnp.stack([grads[0][1], grads[1][1]])
    grad_down = jnp.stack([grads[0][2], grads[1][2]])
    return (section_out, section_grad, grad_gate, grad_up, grad_down)
```

```python
import functools
import math

import jax
import jax.numpy as jnp
from jax import lax
from jax.experimental import pallas as pl
from jax.experimental.pallas import tpu as pltpu
from jax.sharding import PartitionSpec as P

MESH = pl.DeviceIdType.MESH
BF16 = jnp.bfloat16
F32 = jnp.float32
EPS = 1e-05
LANES = 128
LAG_FORWARD = 2
LAG_BACKWARD = 2
LAG_LATE = 1


def dot_nt(a, b):
    return lax.dot_general(a, b, (((1,), (1,)), ((), ())), preferred_element_type=F32)


def dot_tn(a, b):
    return lax.dot_general(a, b, (((0,), (0,)), ((), ())), preferred_element_type=F32)


def fold(block):
    half = block.shape[1] // 2
    return jnp.concatenate([block[:, :half], block[:, half:]], axis=0)


def unfold(block):
    half = block.shape[0] // 2
    return jnp.concatenate([block[:half], block[half:]], axis=1)


def hops(b):
    return (4, 3) if b % 2 == 0 else (3, 4)


def row_column(value, rows):
    high = value.astype(BF16).astype(F32)
    lane = lax.broadcasted_iota(jnp.int32, (rows, LANES), 1)
    return jnp.where(lane == 0, high, jnp.where(lane == 1, value - high, 0.0))


def kernel(
    sizes,
    feed, gate_hbm, up_hbm, down_hbm,
    out_ref, grad_ref, gg_ref, gu_ref, gd_ref,
    w_pair, w_down, feed_in, x_all, g_all,
    part_u, send_u, recv_u, part_v, send_v, recv_v,
    act, scale_r, h_all, d_all,
    core_src, core_dst, slab_src, slab_dst, row_src, fold_src, fold_dst,
    acc_pair, acc_down,
    w_sem, feed_s, feed_r, bcast_s, bcast_r, core_s, core_r,
    rsu_s, rsu_r, rsv_s, rsv_r, agh_s, agh_r, agd_s, agd_r,
    slab_s, slab_r, row_s, fold_s, fold_r,
):
    nb, dp, chips, rows, width, hid, tokens = sizes
    slabs = 2 * chips
    batch = slabs * rows
    chunk = batch // dp
    sec = lax.axis_index("section")
    d = lax.axis_index("dp")
    t = lax.axis_index("tensor")
    k = t // 2
    c = t % 2
    other = 1 - sec
    mine = c * chips + k
    pair = 2 * hid

    def at(**axes):
        return axes

    def turn(base, step, size):
        return lax.rem(base + step + size, size)

    def z_at(step):
        return at(dp=turn(d, step, dp))

    def chip_at(j):
        return at(tensor=turn(k, j, chips) * 2 + c)

    sibling = at(tensor=k * 2 + (1 - c))

    def rcopy(src, dst, ss, rs, dev):
        return pltpu.make_async_remote_copy(
            src_ref=src, dst_ref=dst, send_sem=ss, recv_sem=rs, device_id=dev, device_id_type=MESH
        )

    loads = [
        pltpu.make_async_copy(gate_hbm, w_pair.at[pl.ds(0, hid)], w_sem.at[0]),
        pltpu.make_async_copy(up_hbm, w_pair.at[pl.ds(hid, hid)], w_sem.at[1]),
        pltpu.make_async_copy(down_hbm, w_down, w_sem.at[2]),
    ]
    for load in loads:
        load.start()

    barrier = pltpu.get_barrier_semaphore()
    for j in range(1, dp):
        pl.semaphore_signal(barrier, inc=1, device_id=z_at(j), device_id_type=MESH)
    for j in range(1, chips):
        pl.semaphore_signal(barrier, inc=1, device_id=chip_at(j), device_id_type=MESH)
    for j in range(chips):
        pl.semaphore_signal(
            barrier, inc=1, device_id=at(section=other, **chip_at(j)), device_id_type=MESH
        )
    pl.semaphore_signal(barrier, inc=1, device_id=sibling, device_id_type=MESH)
    pl.semaphore_wait(barrier, dp - 1 + chips - 1 + chips + 1)

    ends = []

    def feed_all():
        for j in range(1, dp):
            to = turn(d, j, dp)
            rcopy(feed.at[to], feed_in.at[d], feed_s.at[0], feed_r.at[d], z_at(j)).start()
        ends.append(
            lambda: rcopy(
                feed_in.at[pl.ds(0, dp - 1)], feed_in.at[pl.ds(0, dp - 1)], feed_s.at[0], feed_r.at[0], z_at(1)
            ).wait_send()
        )
        feed_in[d] = feed[d]

    def feed_slab(way, into, b):
        halves = []
        for source in (2 * b, 2 * b + 1):

            @pl.when(d != source)
            def _():
                rcopy(feed.at[source], feed_in.at[source], feed_s.at[0], feed_r.at[source], z_at(1)).wait_recv()

        for source in (2 * b, 2 * b + 1):
            halves.append(unfold(feed_in[source].astype(F32)))
        into[b, mine] = jnp.concatenate(halves, axis=0).astype(BF16)
        for j in range(1, chips):
            rcopy(
                into.at[b, mine], into.at[b, mine], bcast_s.at[way, b], bcast_r.at[way, b], chip_at(j)
            ).start()
        seven = into.at[b, pl.ds(0, chips - 1)]
        ends.append(lambda: rcopy(seven, seven, bcast_s.at[way, b], bcast_r.at[way, b], z_at(1)).wait_send())

    def slabs_to_core(way, into, count, b):
        some = into.at[b, pl.ds(0, count)]
        rcopy(some, some, bcast_s.at[way, b], bcast_r.at[way, b], z_at(1)).wait_recv()
        own = into.at[b, pl.ds(c * chips, chips)]
        copy = rcopy(own, own, core_s.at[way, b], core_r.at[way, b], sibling)
        copy.start()
        ends.append(copy.wait_send)

    def wait_core(way, into, b):
        rest = into.at[b, pl.ds((1 - c) * chips, chips)]
        rcopy(rest, rest, core_s.at[way, b], core_r.at[way, b], sibling).wait_recv()

    def rs_step(step, part, src, dst, ss, rs, b):
        for way, count in enumerate(hops(b)):
            if step > count:
                continue
            sign = 1 - 2 * way
            at_chunk = turn(d, sign * (count + 1 - step), dp)
            value = part[b, at_chunk]
            if step > 1:
                rcopy(
                    src.at[b, way, step - 2], dst.at[b, way, step - 2], ss.at[b, way, step - 2],
                    rs.at[b, way, step - 2], z_at(sign),
                ).wait_recv()
                value = value + dst[b, way, step - 2].astype(F32)
            src[b, way, step - 1] = value.astype(BF16)
            copy = rcopy(
                src.at[b, way, step - 1], dst.at[b, way, step - 1], ss.at[b, way, step - 1],
                rs.at[b, way, step - 1], z_at(sign),
            )
            copy.start()
            ends.append(copy.wait_send)

    def rs_total(part, src, dst, ss, rs, b):
        total = part[b, d]
        for way, count in enumerate(hops(b)):
            sign = 1 - 2 * way
            rcopy(
                src.at[b, way, count - 1], dst.at[b, way, count - 1], ss.at[b, way, count - 1],
                rs.at[b, way, count - 1], z_at(sign),
            ).wait_recv()
            total = total + dst[b, way, count - 1].astype(F32)
        return total

    def ag_wait(step, buf, ss, rs, way, b):
        sign = 1 - 2 * way
        got = buf.at[b, turn(d, -sign * step, dp)]
        rcopy(got, got, ss.at[b, way, step - 1], rs.at[b, way, step - 1], z_at(sign)).wait_recv()

    def ag_step(step, buf, ss, rs, b):
        for way, count in enumerate(hops(b)):
            if step > count:
                continue
            sign = 1 - 2 * way
            if step > 1:
                ag_wait(step - 1, buf, ss, rs, way, b)
            piece = buf.at[b, turn(d, -sign * (step - 1), dp)]
            copy = rcopy(piece, piece, ss.at[b, way, step - 1], rs.at[b, way, step - 1], z_at(sign))
            copy.start()
            ends.append(copy.wait_send)

    def ag_finish(buf, ss, rs, b):
        for way, count in enumerate(hops(b)):
            ag_wait(count, buf, ss, rs, way, b)

    rs_u = (part_u, send_u, recv_u, rsu_s, rsu_r)
    rs_v = (part_v, send_v, recv_v, rsv_s, rsv_r)
    ag_h = (h_all, agh_s, agh_r)
    ag_d = (d_all, agd_s, agd_r)

    def project_up(b):
        wait_core(0, x_all, b)
        x = x_all[b].reshape(batch, width)
        u = dot_nt(x, w_pair[...])
        xf = x.astype(F32)
        squares = jnp.sum(xf * xf, axis=1, keepdims=True)
        part_u[b, :, :, 0:pair] = u.reshape(dp, chunk, pair)
        part_u[b, :, :, pair:] = row_column(squares, batch).reshape(dp, chunk, LANES)
        rs_step(1, *rs_u, b)

    def project_dh(b):
        wait_core(1, g_all, b)
        g = g_all[b].reshape(batch, width)
        part_v[b] = dot_nt(g, w_down[...]).reshape(dp, chunk, hid)
        rs_step(1, *rs_v, b)

    def hidden(send, b):
        total = rs_total(*rs_u, b)
        squares = jnp.sum(total[:, pair:], axis=1, keepdims=True)
        r = lax.rsqrt(squares / (width * dp) + EPS)
        ab = total[:, :pair] * r
        a, up = ab[:, :hid], ab[:, hid:]
        act[b] = ab
        scale_r[b] = jnp.broadcast_to(r, (chunk, LANES))
        h_all[b, d] = (a * jax.nn.sigmoid(a) * up).astype(BF16)
        if send:
            ag_step(1, *ag_h, b)

    def hidden_grad(b):
        dh = rs_total(*rs_v, b)
        r = scale_r[b][:, 0:1]
        a, up = act[b, :, :hid], act[b, :, hid:]
        sig = jax.nn.sigmoid(a)
        da = (r * (dh * up * sig * (1.0 + a * (1.0 - sig)))).astype(BF16)
        db = (r * (dh * a * sig)).astype(BF16)
        mixed = r * jnp.sum(da.astype(F32) * a + db.astype(F32) * up, axis=1, keepdims=True)
        d_all[b, d, :, 0:hid] = da
        d_all[b, d, :, hid:pair] = db
        d_all[b, d, :, pair:] = row_column(mixed, chunk).astype(BF16)
        ag_step(1, *ag_d, b)

    def to_sibling(way, b):
        rest = core_src.at[way, b, pl.ds((1 - c) * chips, chips)]
        copy = rcopy(rest, core_dst.at[way, b], core_s.at[2 + way, b], core_r.at[2 + way, b], sibling)
        copy.start()
        ends.append(copy.wait_send)

    def project_down(b):
        ag_finish(*ag_h, b)
        h = h_all[b].reshape(batch, hid)
        p = jnp.dot(h, w_down[...], preferred_element_type=F32)
        core_src[0, b] = p.astype(BF16).reshape(slabs, rows, width)
        to_sibling(0, b)

    def project_dn(b):
        ag_finish(*ag_d, b)
        flat = d_all[b].reshape(batch, pair + LANES)
        mixed = jnp.sum(flat[:, pair:].astype(F32), axis=1, keepdims=True)
        q = jnp.dot(flat[:, :pair], w_pair[...], preferred_element_type=F32)
        xf = x_all[b].reshape(batch, width).astype(F32)
        q = q - xf * (mixed * (1.0 / (width * dp)))
        core_src[1, b] = q.astype(BF16).reshape(slabs, rows, width)
        to_sibling(1, b)

    def scatter_slabs(way, b):
        rest = core_dst.at[way, b]
        rcopy(rest, rest, core_s.at[2 + way, b], core_r.at[2 + way, b], sibling).wait_recv()
        both = core_src[way, b, pl.ds(c * chips, chips)].astype(F32) + core_dst[way, b].astype(F32)
        slab_src[way, b] = both.astype(BF16)
        for j in range(1, chips):
            to = turn(k, j, chips)
            rcopy(
                slab_src.at[way, b, to], slab_dst.at[way, b, k], slab_s.at[way, b], slab_r.at[way, b], chip_at(j)
            ).start()
        seven = slab_dst.at[way, b, pl.ds(0, chips - 1)]
        ends.append(lambda: rcopy(seven, seven, slab_s.at[way, b], slab_r.at[way, b], z_at(1)).wait_send())

    def slab_total(way, b):
        seven = slab_dst.at[way, b, pl.ds(0, chips - 1)]
        rcopy(seven, seven, slab_s.at[way, b], slab_r.at[way, b], z_at(1)).wait_recv()
        total = slab_src[way, b, k].astype(F32)
        for j in range(1, chips):
            total = total + slab_dst[way, b, turn(k, j, chips)].astype(F32)
        return total

    def finish_slab(way, value, into, b):
        row_src[way, b] = value.astype(BF16)
        if into is not None:
            for j in range(chips):
                rcopy(
                    row_src.at[way, b], into.at[b, mine], row_s.at[way, b], bcast_r.at[way, b],
                    at(section=other, **chip_at(j)),
                ).start()
            eight = into.at[b, pl.ds(0, chips)]
            ends.append(lambda: rcopy(eight, eight, row_s.at[way, b], bcast_r.at[way, b], z_at(1)).wait_send())
        value = value.astype(BF16).astype(F32)
        half = rows // 2
        for i in range(2):
            owner = 2 * b + i
            fold_src[way, b, i] = fold(value[i * half : (i + 1) * half]).astype(BF16)
            copy = rcopy(
                fold_src.at[way, b, i], fold_dst.at[way, d], fold_s.at[way, b, i], fold_r.at[way], at(dp=owner)
            )

            @pl.when(d == owner)
            def _():
                fold_dst[way, d] = fold_src[way, b, i]

            @pl.when(d != owner)
            def _():
                copy.start()

            def end(copy=copy, owner=owner):
                @pl.when(d != owner)
                def _():
                    copy.wait_send()

            ends.append(end)

    def finish_out(into, b):
        finish_slab(0, x_all[b, mine].astype(F32) + slab_total(0, b), into, b)

    def finish_grad(into, b):
        finish_slab(1, g_all[b, mine].astype(F32) + slab_total(1, b), into, b)

    def weight_grads(b):
        x = x_all[b].reshape(batch, width)
        g = g_all[b].reshape(batch, width)
        pair_part = dot_tn(d_all[b].reshape(batch, pair + LANES)[:, :pair], x)
        down_part = dot_tn(h_all[b].reshape(batch, hid), g)
        if b == 0:
            acc_pair[...] = pair_part
            acc_down[...] = down_part
        else:
            acc_pair[...] += pair_part
            acc_down[...] += down_part

    def collect(way, ref):
        seven = fold_dst.at[way, pl.ds(0, dp - 1)]
        rcopy(seven, seven, fold_s.at[way, 0, 0], fold_r.at[way], z_at(1)).wait_recv()
        for source in range(dp):
            ref[:, source * width : (source + 1) * width] = unfold(fold_dst[way, source].astype(F32))

    def wave(ops, lag):
        for tick in range(len(ops) + lag * (nb - 1)):
            for b in range(nb):
                index = tick - lag * b
                if 0 <= index < len(ops):
                    ops[index](b)

    def part(function, *args):
        return functools.partial(function, *args)

    def rs_ops(which):
        return [part(rs_step, step, *which) for step in (2, 3, 4)]

    def ag_ops(which):
        return [part(ag_step, step, *which) for step in (2, 3, 4)]

    def both(*functions):
        def run(b):
            for function in functions:
                function(b)

        return run

    def wait_weights():
        for load in loads:
            load.wait()

    def close():
        scale = 1.0 / math.sqrt(tokens)
        gg_ref[...] = (acc_pair[0:hid] * scale).astype(BF16)
        gu_ref[...] = (acc_pair[hid:pair] * scale).astype(BF16)
        gd_ref[...] = (acc_down[...] * scale).astype(BF16)
        collect(0, out_ref)
        collect(1, grad_ref)
        for end in ends:
            end()
        ends.clear()

    feed_all()
    shared = list(ends)

    @pl.when(sec == 0)
    def _():
        ends[:] = shared
        wait_weights()
        wave(
            [
                part(feed_slab, 0, x_all),
                part(slabs_to_core, 0, x_all, chips - 1),
                project_up,
                *rs_ops(rs_u),
                part(hidden, True),
                *ag_ops(ag_h),
                project_down,
                part(scatter_slabs, 0),
                part(finish_out, x_all),
            ],
            LAG_FORWARD,
        )
        wave(
            [
                part(slabs_to_core, 1, g_all, chips),
                project_dh,
                *rs_ops(rs_v),
                hidden_grad,
                *ag_ops(ag_d),
                project_dn,
                part(scatter_slabs, 1),
                both(weight_grads, part(finish_grad, None)),
            ],
            LAG_BACKWARD,
        )
        close()

    @pl.when(sec == 1)
    def _():
        ends[:] = shared
        wait_weights()
        wave(
            [
                part(feed_slab, 1, g_all),
                part(slabs_to_core, 1, g_all, chips - 1),
                project_dh,
                *rs_ops(rs_v),
            ],
            1,
        )
        wave(
            [
                part(slabs_to_core, 0, x_all, chips),
                project_up,
                *rs_ops(rs_u),
                both(part(hidden, False), hidden_grad),
                *ag_ops(ag_d),
                project_dn,
                part(scatter_slabs, 1),
                part(finish_grad, g_all),
            ],
            LAG_BACKWARD,
        )
        wave(
            [
                part(ag_step, 1, *ag_h),
                *ag_ops(ag_h),
                project_down,
                part(scatter_slabs, 0),
                both(weight_grads, part(finish_out, None)),
            ],
            LAG_LATE,
        )
        close()


def shards(inputs, cotangent, gate_weight, up_weight, down_weight):
    first = lax.axis_index("section") == 0
    dp, tensors = lax.axis_size("dp"), lax.axis_size("tensor")
    micro, tok_dev, model = inputs.shape
    _, hid, width = gate_weight.shape
    chips = tensors // 2
    share = tok_dev // tensors
    held = micro * share
    nb, rows = dp // 2, 2 * held
    batch = tensors * rows
    chunk = batch // dp
    pair = 2 * hid
    start = lax.axis_index("tensor") * share
    pick = jnp.where(
        first,
        lax.dynamic_slice_in_dim(inputs, start, share, 1),
        lax.dynamic_slice_in_dim(cotangent, start, share, 1),
    )
    feed = pick.reshape(held, dp, 2, width // 2).transpose(1, 2, 0, 3).reshape(dp, rows, width // 2)

    def sems(*shape):
        return pltpu.SemaphoreType.DMA(shape)

    def bf16(*shape):
        return pltpu.VMEM(shape, BF16)

    def f32(*shape):
        return pltpu.VMEM(shape, F32)

    sizes = (nb, dp, chips, rows, width, hid, micro * tok_dev * dp)
    vmem = pl.BlockSpec(memory_space=pltpu.VMEM)
    anywhere = pl.BlockSpec(memory_space=pl.ANY)
    out, grad, grad_gate, grad_up, grad_down = pl.pallas_call(
        functools.partial(kernel, sizes),
        out_shape=[
            jax.ShapeDtypeStruct((held, model), F32),
            jax.ShapeDtypeStruct((held, model), F32),
            jax.ShapeDtypeStruct((hid, width), BF16),
            jax.ShapeDtypeStruct((hid, width), BF16),
            jax.ShapeDtypeStruct((hid, width), BF16),
        ],
        in_specs=[vmem, anywhere, anywhere, anywhere],
        out_specs=[vmem] * 5,
        scratch_shapes=[
            bf16(pair, width),
            bf16(hid, width),
            bf16(dp, rows, width // 2),
            bf16(nb, tensors, rows, width),
            bf16(nb, tensors, rows, width),
            f32(nb, dp, chunk, pair + LANES),
            bf16(nb, 2, 4, chunk, pair + LANES),
            bf16(nb, 2, 4, chunk, pair + LANES),
            f32(nb, dp, chunk, hid),
            bf16(nb, 2, 4, chunk, hid),
            bf16(nb, 2, 4, chunk, hid),
            f32(nb, chunk, pair),
            f32(nb, chunk, LANES),
            bf16(nb, dp, chunk, hid),
            bf16(nb, dp, chunk, pair + LANES),
            bf16(2, nb, tensors, rows, width),
            bf16(2, nb, chips, rows, width),
            bf16(2, nb, chips, rows, width),
            bf16(2, nb, chips, rows, width),
            bf16(2, nb, rows, width),
            bf16(2, nb, 2, rows, width // 2),
            bf16(2, dp, rows, width // 2),
            f32(pair, width),
            f32(hid, width),
            sems(3),
            sems(1),
            sems(dp),
            sems(2, nb),
            sems(2, nb),
            sems(4, nb),
            sems(4, nb),
            *[sems(nb, 2, 4) for _ in range(8)],
            sems(2, nb),
            sems(2, nb),
            sems(2, nb),
            sems(2, nb, 2),
            sems(2),
        ],
        compiler_params=pltpu.CompilerParams(
            collective_id=0, has_side_effects=True, vmem_limit_bytes=56 * 1024 * 1024
        ),
    )(feed, gate_weight[0], up_weight[0], down_weight[0])
    section_out = out.astype(BF16).reshape(1, micro, share, model)
    section_grad = grad.astype(BF16).reshape(1, micro, share, model)
    return (section_out, section_grad, grad_gate[None], grad_up[None], grad_down[None])


def solution(mesh):
    in_specs = (
        P(None, "dp", None),
        P(None, "dp", None),
        P("section", "tensor", "dp"),
        P("section", "tensor", "dp"),
        P("section", "tensor", "dp"),
    )
    out_specs = (
        P("section", None, ("dp", "tensor"), None),
        P("section", None, ("dp", "tensor"), None),
        P("section", "tensor", "dp"),
        P("section", "tensor", "dp"),
        P("section", "tensor", "dp"),
    )
    return jax.shard_map(shards, mesh=mesh, in_specs=in_specs, out_specs=out_specs, check_vma=False)
```

```python
import functools
import math

import jax
import jax.numpy as jnp
from jax import lax
from jax.experimental import pallas as pl
from jax.experimental.pallas import tpu as pltpu
from jax.sharding import PartitionSpec as P

MESH = pl.DeviceIdType.MESH
BF16 = jnp.bfloat16
F32 = jnp.float32
EPS = 1e-05
LANES = 128
ORDER_FIRST = (
    (0, 0), (0, 1), (0, 2), (0, 3), (0, 4), (0, 5), (0, 6), (0, 7), (1, 0), (1, 1), (2, 0), (2, 1), (1, 2), (1, 3), (2, 2),
    (2, 3), (1, 4), (3, 0), (1, 5), (3, 1), (2, 4), (1, 6), (2, 5), (2, 6), (3, 2), (1, 7), (3, 3), (2, 7), (4, 0), (4, 1),
    (3, 4), (3, 5), (3, 6), (4, 2), (4, 3), (3, 7), (5, 0), (5, 1), (4, 4), (4, 5), (4, 6), (5, 3), (5, 2), (4, 7), (6, 0),
    (6, 1), (5, 4), (5, 6), (5, 5), (5, 7), (6, 2), (6, 3), (6, 5), (11, 0), (12, 0), (6, 4), (6, 7), (6, 6), (11, 1), (12, 1),
    (11, 2), (12, 2), (13, 0), (11, 3), (12, 3), (13, 1), (11, 5), (12, 5), (13, 2), (11, 4), (12, 4), (11, 7), (13, 3),
    (12, 7), (13, 5), (11, 6), (12, 6), (13, 4), (13, 7), (13, 6), (14, 1), (15, 1), (14, 0), (15, 0), (16, 1), (14, 2),
    (16, 0), (15, 2), (14, 3), (19, 1), (15, 3), (14, 5), (19, 0), (16, 2), (14, 7), (15, 5), (15, 7), (14, 4), (20, 1),
    (15, 4), (16, 3), (20, 0), (14, 6), (19, 2), (15, 6), (16, 5), (16, 7), (21, 1), (16, 4), (19, 3), (21, 0), (20, 2),
    (16, 6), (19, 5), (22, 1), (19, 7), (20, 3), (19, 4), (22, 0), (21, 2), (19, 6), (23, 1), (20, 5), (20, 7), (24, 1),
    (20, 4), (21, 3), (23, 0), (26, 0), (26, 1), (22, 2), (24, 0), (20, 6), (21, 5), (21, 7), (21, 4), (22, 3), (25, 1),
    (21, 6), (23, 2), (22, 5), (26, 2), (22, 7), (22, 4), (25, 0), (24, 2), (23, 3), (26, 3), (22, 6), (24, 3), (23, 5),
    (23, 7), (23, 4), (24, 5), (24, 7), (26, 4), (26, 5), (23, 6), (24, 4), (25, 2), (26, 6), (24, 6), (26, 7), (25, 3),
    (25, 5), (25, 4), (25, 7), (25, 6),
)
ORDER_SECOND = (
    (0, 1), (0, 0), (0, 2), (0, 3), (0, 4), (0, 5), (0, 6), (0, 7), (14, 0), (15, 0), (14, 1), (15, 1), (14, 2), (14, 4),
    (14, 3), (15, 2), (15, 3), (14, 5), (15, 4), (16, 0), (14, 7), (15, 5), (16, 1), (14, 6), (15, 6), (16, 2), (16, 3),
    (15, 7), (16, 4), (16, 6), (16, 5), (1, 0), (16, 7), (2, 0), (1, 1), (2, 1), (1, 2), (3, 0), (2, 2), (3, 1), (1, 3),
    (2, 3), (4, 0), (3, 2), (1, 5), (4, 1), (2, 5), (1, 4), (3, 3), (5, 0), (2, 4), (1, 7), (4, 2), (5, 1), (2, 7), (3, 5),
    (1, 6), (4, 3), (6, 0), (19, 0), (2, 6), (3, 4), (6, 1), (19, 1), (5, 2), (3, 7), (4, 5), (5, 3), (20, 0), (3, 6), (4, 4),
    (20, 1), (6, 2), (19, 2), (4, 7), (5, 5), (21, 0), (6, 3), (19, 3), (4, 6), (5, 4), (21, 1), (5, 7), (20, 2), (6, 5),
    (19, 5), (20, 3), (5, 6), (22, 0), (22, 1), (6, 4), (19, 4), (6, 7), (19, 7), (21, 2), (20, 5), (21, 3), (6, 6), (19, 6),
    (23, 1), (20, 4), (23, 0), (20, 7), (24, 1), (24, 0), (22, 2), (21, 5), (22, 3), (20, 6), (21, 4), (21, 7), (23, 2),
    (22, 5), (25, 1), (24, 2), (21, 6), (23, 3), (25, 0), (22, 4), (22, 7), (24, 3), (23, 5), (22, 6), (24, 5), (23, 4),
    (23, 7), (25, 2), (7, 0), (7, 1), (7, 2), (7, 3), (7, 4), (24, 7), (7, 5), (7, 7), (7, 6), (24, 4), (23, 6), (25, 3),
    (24, 6), (25, 5), (8, 0), (8, 1), (8, 2), (8, 4), (8, 3), (8, 5), (25, 7), (8, 6), (8, 7), (9, 0), (9, 1), (9, 2), (25, 4),
    (9, 4), (9, 3), (9, 5), (9, 6), (9, 7), (25, 6), (10, 1), (10, 0), (10, 2), (10, 4), (10, 7), (10, 5), (10, 3), (10, 6),
    (11, 1), (11, 2), (26, 2), (11, 0), (26, 0), (26, 1), (12, 0), (12, 1), (12, 2), (11, 3), (26, 3), (12, 3), (11, 4),
    (26, 4), (11, 5), (26, 5), (12, 4), (12, 5), (11, 6), (12, 6), (26, 6), (13, 4), (11, 7), (26, 7), (13, 0), (12, 7),
    (13, 1), (13, 2), (13, 3), (13, 5), (13, 6), (13, 7),
)


def dot_nt(a, b):
    return lax.dot_general(a, b, (((1,), (1,)), ((), ())), preferred_element_type=F32)


def dot_tn(a, b):
    return lax.dot_general(a, b, (((0,), (0,)), ((), ())), preferred_element_type=F32)


RING, PAIRS, DIRECT = 0, 1, 2
PARENT = ((0, 1, 2, 3), (0, 0, 2, 2), (0, 0, 0, 0))
ROUTES_FIRST = {
    "u": (RING,) * 8,
    "h": (DIRECT,) * 8,
    "v": (PAIRS,) * 8,
    "d": (RING,) * 8,
}
ROUTES_SECOND = {
    "u": (RING,) * 8,
    "h": (RING,) * 8,
    "v": (PAIRS,) * 8,
    "d": (RING,) * 8,
}


def hops(b):
    return (4, 3) if b % 2 == 0 else (3, 4)


def legs(kind, b, stage):
    pairs = []
    for way, count in enumerate(hops(b)):
        if kind == RING:
            some = [count + 1 - stage]
        elif kind == PAIRS:
            some = [(3, 4, 1), (2,)][stage - 1]
        else:
            some = (3, 4, 2, 1)
        pairs += [(way, s) for s in some if 1 <= s <= count]
    return pairs


def children(kind, count, s):
    return [later for later in range(s + 1, count + 1) if PARENT[kind][later - 1] == s]


def waited(kind, s):
    return (kind == RING and s <= 3) or (kind == PAIRS and s == 2)


def row_column(value, rows):
    high = value.astype(BF16).astype(F32)
    lane = lax.broadcasted_iota(jnp.int32, (rows, LANES), 1)
    return jnp.where(lane == 0, high, jnp.where(lane == 1, value - high, 0.0))


def kernel(
    sizes,
    feed, gate_hbm, up_hbm, down_hbm,
    out_ref, grad_ref, gg_ref, gu_ref, gd_ref,
    w_pair, w_down, x_all, g_all,
    part_u, send_u, recv_u, part_v, send_v, recv_v,
    act, scale_r, h_all, d_all,
    core_src, core_dst, slab_src, slab_dst, row_src, out_dst,
    acc_pair, acc_down,
    w_sem, feed_s, feed_r, bcast_s, bcast_r, core_s, core_r,
    rsu_s, rsu_r, rsv_s, rsv_r, agh_s, agh_r, agd_s, agd_r,
    slab_s, slab_r, row_s, out_s, out_r,
):
    nb, dp, chips, rows, width, hid, tokens = sizes
    half = width // 2
    batch = chips * rows
    chunk = batch // dp
    sec = lax.axis_index("section")
    d = lax.axis_index("dp")
    t = lax.axis_index("tensor")
    k = t // 2
    c = t % 2
    other = 1 - sec
    pair = 2 * hid

    def at(**axes):
        return axes

    def turn(base, step, size):
        return lax.rem(base + step + size, size)

    def z_at(step):
        return at(dp=turn(d, step, dp))

    def chip_at(j):
        return at(tensor=turn(k, j, chips) * 2 + c)

    sibling = at(tensor=k * 2 + (1 - c))

    def rcopy(src, dst, ss, rs, dev):
        return pltpu.make_async_remote_copy(
            src_ref=src, dst_ref=dst, send_sem=ss, recv_sem=rs, device_id=dev, device_id_type=MESH
        )

    loads = [
        pltpu.make_async_copy(gate_hbm, w_pair.at[pl.ds(0, hid)], w_sem.at[0]),
        pltpu.make_async_copy(up_hbm, w_pair.at[pl.ds(hid, hid)], w_sem.at[1]),
        pltpu.make_async_copy(down_hbm, w_down, w_sem.at[2]),
    ]
    for load in loads:
        load.start()

    barrier = pltpu.get_barrier_semaphore()
    for j in range(1, dp):
        pl.semaphore_signal(barrier, inc=1, device_id=z_at(j), device_id_type=MESH)
    for j in range(1, chips):
        pl.semaphore_signal(barrier, inc=1, device_id=chip_at(j), device_id_type=MESH)
    for j in range(chips):
        pl.semaphore_signal(
            barrier, inc=1, device_id=at(section=other, **chip_at(j)), device_id_type=MESH
        )
    for j in range(dp):
        pl.semaphore_signal(barrier, inc=1, device_id={**z_at(j), **sibling}, device_id_type=MESH)
    pl.semaphore_wait(barrier, dp - 1 + chips - 1 + chips + dp)

    ends = []

    def feed_all(into):
        for j in range(1, dp):
            rcopy(
                feed.at[turn(d, j, dp)], into.at[d, c, k], feed_s.at[0], feed_r.at[d], z_at(j)
            ).start()
        seven = feed.at[pl.ds(0, dp - 1)]
        ends.append(lambda: rcopy(seven, seven, feed_s.at[0], feed_r.at[0], z_at(1)).wait_send())
        into[d, c, k] = feed[d]

    def feed_slab(way, into, b):
        @pl.when(d != b)
        def _():
            rcopy(into.at[b, c, k], into.at[b, c, k], feed_s.at[0], feed_r.at[b], z_at(1)).wait_recv()

        for j in range(1, chips):
            rcopy(
                into.at[b, c, k], into.at[b, c, k], bcast_s.at[way, b], bcast_r.at[way, b], chip_at(j)
            ).start()
        seven = into.at[b, c, pl.ds(0, chips - 1)]
        ends.append(lambda: rcopy(seven, seven, bcast_s.at[way, b], bcast_r.at[way, b], z_at(1)).wait_send())

    def slabs_to_core(way, into, count, b):
        some = into.at[b, c, pl.ds(0, count)]
        rcopy(some, some, bcast_s.at[way, b], bcast_r.at[way, b], z_at(1)).wait_recv()
        own = into.at[b, c]
        copy = rcopy(own, own, core_s.at[way, b], core_r.at[way, b], sibling)
        copy.start()
        ends.append(copy.wait_send)

    def wait_core(way, into, b):
        rest = into.at[b, 1 - c]
        rcopy(rest, rest, core_s.at[way, b], core_r.at[way, b], sibling).wait_recv()

    def rs_copy(kind, way, s, src, dst, ss, rs, b):
        hop = (1 - 2 * way) * (s - PARENT[kind][s - 1])
        at_leg = (b, way, s - 1)
        return rcopy(src.at[at_leg], dst.at[at_leg], ss.at[at_leg], rs.at[at_leg], z_at(hop))

    def rs_step(stage, which, part, src, dst, ss, rs, b):
        kind = which[b]
        for way, s in legs(kind, b, stage):
            value = part[b, turn(d, (1 - 2 * way) * s, dp)]
            for later in children(kind, hops(b)[way], s):
                rs_copy(kind, way, later, src, dst, ss, rs, b).wait_recv()
                value = value + dst[b, way, later - 1].astype(F32)
            src[b, way, s - 1] = value.astype(BF16)
            copy = rs_copy(kind, way, s, src, dst, ss, rs, b)
            copy.start()
            ends.append(copy.wait_send)

    def rs_total(which, part, src, dst, ss, rs, b):
        kind = which[b]
        total = part[b, d]
        for way, count in enumerate(hops(b)):
            for s in children(kind, count, 0):
                rs_copy(kind, way, s, src, dst, ss, rs, b).wait_recv()
                total = total + dst[b, way, s - 1].astype(F32)
        return total

    def ag_copy(kind, way, s, buf, ss, rs, b, held):
        sign = 1 - 2 * way
        piece = buf.at[b, turn(d, -sign * held, dp)]
        return rcopy(
            piece, piece, ss.at[b, way, s - 1], rs.at[b, way, s - 1], z_at(sign * (s - PARENT[kind][s - 1]))
        )

    def ag_step(stage, which, buf, ss, rs, b):
        kind = which[b]
        held = 2 if kind == PAIRS and stage == 2 else stage - 1
        order = (3, 4, 2, 1) if held == 0 else (4, 3, 2, 1)
        for way, count in enumerate(hops(b)):
            if held:
                ag_copy(kind, way, held, buf, ss, rs, b, held).wait_recv()
            later = children(kind, count, held)
            for s in order:
                if s in later:
                    copy = ag_copy(kind, way, s, buf, ss, rs, b, held)
                    copy.start()
                    ends.append(copy.wait_send)

    def ag_finish(which, buf, ss, rs, b):
        kind = which[b]
        for way, count in enumerate(hops(b)):
            for s in range(1, count + 1):
                if not waited(kind, s):
                    ag_copy(kind, way, s, buf, ss, rs, b, s).wait_recv()

    routes = {}

    def rs_u():
        return (routes["u"], part_u, send_u, recv_u, rsu_s, rsu_r)

    def rs_v():
        return (routes["v"], part_v, send_v, recv_v, rsv_s, rsv_r)

    def ag_h():
        return (routes["h"], h_all, agh_s, agh_r)

    def ag_d():
        return (routes["d"], d_all, agd_s, agd_r)

    def whole(ref, b, count=1):
        parts = [ref[b : b + count, i].reshape(count * batch, half) for i in range(2)]
        return jnp.concatenate(parts, axis=1)

    def project_up(b):
        wait_core(0, x_all, b)
        x = whole(x_all, b)
        u = dot_nt(x, w_pair[...])
        xf = x.astype(F32)
        squares = jnp.sum(xf * xf, axis=1, keepdims=True)
        part_u[b, :, :, 0:pair] = u.reshape(dp, chunk, pair)
        part_u[b, :, :, pair:] = row_column(squares, batch).reshape(dp, chunk, LANES)
        rs_step(1, *rs_u(), b)

    def project_dh(b):
        wait_core(1, g_all, b)
        g = whole(g_all, b)
        part_v[b] = dot_nt(g, w_down[...]).reshape(dp, chunk, hid)
        rs_step(1, *rs_v(), b)

    def hidden(send, b):
        total = rs_total(*rs_u(), b)
        squares = jnp.sum(total[:, pair:], axis=1, keepdims=True)
        r = lax.rsqrt(squares / (width * dp) + EPS)
        ab = total[:, :pair] * r
        a, up = ab[:, :hid], ab[:, hid:]
        act[b] = ab
        scale_r[b] = jnp.broadcast_to(r, (chunk, LANES))
        h_all[b, d] = (a * jax.nn.sigmoid(a) * up).astype(BF16)
        if send:
            ag_step(1, *ag_h(), b)

    def hidden_grad(b):
        dh = rs_total(*rs_v(), b)
        r = scale_r[b][:, 0:1]
        a, up = act[b, :, :hid], act[b, :, hid:]
        sig = jax.nn.sigmoid(a)
        da = (r * (dh * up * sig * (1.0 + a * (1.0 - sig)))).astype(BF16)
        db = (r * (dh * a * sig)).astype(BF16)
        mixed = r * jnp.sum(da.astype(F32) * a + db.astype(F32) * up, axis=1, keepdims=True)
        d_all[b, d, :, 0:hid] = da
        d_all[b, d, :, hid:pair] = db
        d_all[b, d, :, pair:] = row_column(mixed, chunk).astype(BF16)
        ag_step(1, *ag_d(), b)

    def to_sibling(way, b):
        rest = core_src.at[way, b, 1 - c]
        copy = rcopy(rest, core_dst.at[way, b], core_s.at[2 + way, b], core_r.at[2 + way, b], sibling)
        copy.start()
        ends.append(copy.wait_send)

    def halves_out(way, value, b):
        for i in range(2):
            core_src[way, b, i] = value[:, i * half : (i + 1) * half].astype(BF16).reshape(chips, rows, half)

    def project_down(b):
        ag_finish(*ag_h(), b)
        h = h_all[b].reshape(batch, hid)
        p = jnp.dot(h, w_down[...], preferred_element_type=F32)
        halves_out(0, p, b)
        to_sibling(0, b)

    def project_dn(b):
        ag_finish(*ag_d(), b)
        flat = d_all[b].reshape(batch, pair + LANES)
        mixed = jnp.sum(flat[:, pair:].astype(F32), axis=1, keepdims=True)
        q = jnp.dot(flat[:, :pair], w_pair[...], preferred_element_type=F32)
        xf = whole(x_all, b).astype(F32)
        q = q - xf * (mixed * (1.0 / (width * dp)))
        halves_out(1, q, b)
        to_sibling(1, b)

    def scatter_slabs(way, b):
        rest = core_dst.at[way, b]
        rcopy(rest, rest, core_s.at[2 + way, b], core_r.at[2 + way, b], sibling).wait_recv()
        both = core_src[way, b, c].astype(F32) + core_dst[way, b].astype(F32)
        slab_src[way, b] = both.astype(BF16)
        for j in range(1, chips):
            to = turn(k, j, chips)
            rcopy(
                slab_src.at[way, b, to], slab_dst.at[way, b, k], slab_s.at[way, b], slab_r.at[way, b], chip_at(j)
            ).start()
        seven = slab_dst.at[way, b, pl.ds(0, chips - 1)]
        ends.append(lambda: rcopy(seven, seven, slab_s.at[way, b], slab_r.at[way, b], z_at(1)).wait_send())

    def slab_total(way, b):
        seven = slab_dst.at[way, b, pl.ds(0, chips - 1)]
        rcopy(seven, seven, slab_s.at[way, b], slab_r.at[way, b], z_at(1)).wait_recv()
        total = slab_src[way, b, k].astype(F32)
        for j in range(1, chips):
            total = total + slab_dst[way, b, turn(k, j, chips)].astype(F32)
        return total

    def finish_slab(way, value, into, b):
        row_src[way, b] = value.astype(BF16)
        if into is not None:
            for j in range(chips):
                rcopy(
                    row_src.at[way, b], into.at[b, c, k], row_s.at[way, b], bcast_r.at[way, b],
                    at(section=other, **chip_at(j)),
                ).start()
            eight = into.at[b, c]
            ends.append(lambda: rcopy(eight, eight, row_s.at[way, b], bcast_r.at[way, b], z_at(1)).wait_send())
        source = d * 2 + c
        crossed = rcopy(
            row_src.at[way, b], out_dst.at[way, source], out_s.at[way, b, 1], out_r.at[way], {"dp": b, **sibling}
        )
        crossed.start()
        ends.append(crossed.wait_send)
        copy = rcopy(row_src.at[way, b], out_dst.at[way, source], out_s.at[way, b, 0], out_r.at[way], at(dp=b))

        @pl.when(d == b)
        def _():
            out_dst[way, source] = row_src[way, b]

        @pl.when(d != b)
        def _():
            copy.start()

        def end():
            @pl.when(d != b)
            def _():
                copy.wait_send()

        ends.append(end)

    def finish_out(into, b):
        finish_slab(0, x_all[b, c, k].astype(F32) + slab_total(0, b), into, b)

    def finish_grad(into, b):
        finish_slab(1, g_all[b, c, k].astype(F32) + slab_total(1, b), into, b)

    def weight_grads(b):
        if b % 2 == 0:
            return
        x = whole(x_all, b - 1, 2)
        g = whole(g_all, b - 1, 2)
        pair_part = dot_tn(d_all[b - 1 : b + 1].reshape(2 * batch, pair + LANES)[:, :pair], x)
        down_part = dot_tn(h_all[b - 1 : b + 1].reshape(2 * batch, hid), g)
        if b == 1:
            acc_pair[...] = pair_part
            acc_down[...] = down_part
        else:
            acc_pair[...] += pair_part
            acc_down[...] += down_part

    def collect(way, ref):
        rest = out_dst.at[way, pl.ds(0, 2 * dp - 1)]
        rcopy(rest, rest, out_s.at[way, 0, 0], out_r.at[way], z_at(1)).wait_recv()
        for source in range(2 * dp):
            block = out_dst[way, source].astype(F32)
            ref[:, source * half : (source + 1) * half] = jnp.where(c == 0, block[: rows // 2], block[rows // 2 :])

    def part(function, *args):
        return functools.partial(function, *args)

    def wait_weights():
        for load in loads:
            load.wait()

    def close():
        scale = 1.0 / math.sqrt(tokens)
        gg_ref[...] = (acc_pair[0:hid] * scale).astype(BF16)
        gu_ref[...] = (acc_pair[hid:pair] * scale).astype(BF16)
        gd_ref[...] = (acc_down[...] * scale).astype(BF16)
        collect(0, out_ref)
        collect(1, grad_ref)
        for end in ends:
            end()
        ends.clear()

    def run(order, kinds, x_slabs, g_slabs, feed_op, hidden_op, out_op, grad_op):
        routes.update(kinds)
        ops = [
            feed_op,
            part(slabs_to_core, 0, x_all, x_slabs),
            project_up,
            *[part(rs_step, step, *rs_u()) for step in (2, 3, 4)],
            hidden_op,
            *[part(ag_step, step, *ag_h()) for step in (1, 2, 3, 4)],
            project_down,
            part(scatter_slabs, 0),
            out_op,
            part(slabs_to_core, 1, g_all, g_slabs),
            project_dh,
            *[part(rs_step, step, *rs_v()) for step in (2, 3, 4)],
            hidden_grad,
            *[part(ag_step, step, *ag_d()) for step in (2, 3, 4)],
            project_dn,
            part(scatter_slabs, 1),
            grad_op,
            weight_grads,
        ]
        for op, b in order:
            ops[op](b)

    @pl.when(sec == 0)
    def _():
        feed_all(x_all)
        wait_weights()
        run(
            ORDER_FIRST, ROUTES_FIRST, chips - 1, chips, part(feed_slab, 0, x_all), part(hidden, True),
            part(finish_out, x_all), part(finish_grad, None),
        )
        close()

    @pl.when(sec == 1)
    def _():
        feed_all(g_all)
        wait_weights()
        run(
            ORDER_SECOND, ROUTES_SECOND, chips, chips - 1, part(feed_slab, 1, g_all), part(hidden, False),
            part(finish_out, None), part(finish_grad, g_all),
        )
        close()


def finish_kernel(out_in, grad_in, gg_in, gu_in, gd_in, out_ref, grad_ref, gg_ref, gu_ref, gd_ref):
    share = out_ref.shape[2]
    for src, dst in ((out_in, out_ref), (grad_in, grad_ref)):
        for m in range(out_ref.shape[1]):
            dst[0, m] = src[m * share : (m + 1) * share].astype(BF16)
    for src, dst in ((gg_in, gg_ref), (gu_in, gu_ref), (gd_in, gd_ref)):
        dst[0] = src[...]


def shards(inputs, cotangent, gate_weight, up_weight, down_weight):
    first = lax.axis_index("section") == 0
    dp, tensors = lax.axis_size("dp"), lax.axis_size("tensor")
    micro, tok_dev, model = inputs.shape
    _, hid, width = gate_weight.shape
    chips = tensors // 2
    share = tok_dev // tensors
    held = micro * share
    nb, rows, half = dp, 2 * held, width // 2
    chunk = chips * rows // dp
    pair = 2 * hid
    tensor = lax.axis_index("tensor")
    start = tensor // 2 * (2 * share)
    pick = jnp.where(
        first,
        lax.dynamic_slice_in_dim(inputs, start, 2 * share, 1),
        lax.dynamic_slice_in_dim(cotangent, start, 2 * share, 1),
    )
    pick = pick.reshape(micro, 2, share, dp, 2, half)
    pick = jnp.where(tensor % 2 == 0, pick[:, :, :, :, 0], pick[:, :, :, :, 1])
    feed = pick.transpose(3, 1, 0, 2, 4).reshape(dp, rows, half)

    def sems(*shape):
        return pltpu.SemaphoreType.DMA(shape)

    def bf16(*shape):
        return pltpu.VMEM(shape, BF16)

    def f32(*shape):
        return pltpu.VMEM(shape, F32)

    sizes = (nb, dp, chips, rows, width, hid, micro * tok_dev * dp)
    vmem = pl.BlockSpec(memory_space=pltpu.VMEM)
    anywhere = pl.BlockSpec(memory_space=pl.ANY)
    out, grad, grad_gate, grad_up, grad_down = pl.pallas_call(
        functools.partial(kernel, sizes),
        out_shape=[
            jax.ShapeDtypeStruct((held, model), F32),
            jax.ShapeDtypeStruct((held, model), F32),
            jax.ShapeDtypeStruct((hid, width), BF16),
            jax.ShapeDtypeStruct((hid, width), BF16),
            jax.ShapeDtypeStruct((hid, width), BF16),
        ],
        in_specs=[vmem, anywhere, anywhere, anywhere],
        out_specs=[vmem] * 5,
        scratch_shapes=[
            bf16(pair, width),
            bf16(hid, width),
            bf16(nb, 2, chips, rows, half),
            bf16(nb, 2, chips, rows, half),
            f32(nb, dp, chunk, pair + LANES),
            bf16(nb, 2, 4, chunk, pair + LANES),
            bf16(nb, 2, 4, chunk, pair + LANES),
            f32(nb, dp, chunk, hid),
            bf16(nb, 2, 4, chunk, hid),
            bf16(nb, 2, 4, chunk, hid),
            f32(nb, chunk, pair),
            f32(nb, chunk, LANES),
            bf16(nb, dp, chunk, hid),
            bf16(nb, dp, chunk, pair + LANES),
            bf16(2, nb, 2, chips, rows, half),
            bf16(2, nb, chips, rows, half),
            bf16(2, nb, chips, rows, half),
            bf16(2, nb, chips, rows, half),
            bf16(2, nb, rows, half),
            bf16(2, 2 * dp, rows, half),
            f32(pair, width),
            f32(hid, width),
            sems(3),
            sems(1),
            sems(dp),
            sems(2, nb),
            sems(2, nb),
            sems(4, nb),
            sems(4, nb),
            *[sems(nb, 2, 4) for _ in range(8)],
            sems(2, nb),
            sems(2, nb),
            sems(2, nb),
            sems(2, nb, 2),
            sems(2),
        ],
        compiler_params=pltpu.CompilerParams(
            collective_id=0, has_side_effects=True, vmem_limit_bytes=56 * 1024 * 1024
        ),
    )(feed, gate_weight[0], up_weight[0], down_weight[0])
    return pl.pallas_call(
        finish_kernel,
        out_shape=[
            jax.ShapeDtypeStruct((1, micro, share, model), BF16),
            jax.ShapeDtypeStruct((1, micro, share, model), BF16),
            jax.ShapeDtypeStruct((1, hid, width), BF16),
            jax.ShapeDtypeStruct((1, hid, width), BF16),
            jax.ShapeDtypeStruct((1, hid, width), BF16),
        ],
        in_specs=[vmem] * 5,
        out_specs=[vmem] * 5,
    )(out, grad, grad_gate, grad_up, grad_down)


def solution(mesh):
    in_specs = (
        P(None, "dp", None),
        P(None, "dp", None),
        P("section", "tensor", "dp"),
        P("section", "tensor", "dp"),
        P("section", "tensor", "dp"),
    )
    out_specs = (
        P("section", None, ("dp", "tensor"), None),
        P("section", None, ("dp", "tensor"), None),
        P("section", "tensor", "dp"),
        P("section", "tensor", "dp"),
        P("section", "tensor", "dp"),
    )
    return jax.shard_map(shards, mesh=mesh, in_specs=in_specs, out_specs=out_specs, check_vma=False)
```

```python
import functools
import math

import jax
import jax.numpy as jnp
from jax import lax
from jax.experimental import pallas as pl
from jax.experimental.pallas import tpu as pltpu
from jax.sharding import PartitionSpec as P

MESH = pl.DeviceIdType.MESH
BF16 = jnp.bfloat16
F32 = jnp.float32
EPS = 1e-05
LANES = 128
ORDER_FIRST = (
    (0, 0), (0, 1), (0, 2), (0, 3), (0, 4), (0, 5), (0, 6), (0, 7), (1, 0), (1, 1), (2, 0), (2, 1), (1, 2), (1, 3), (2, 2),
    (2, 3), (1, 4), (3, 0), (1, 5), (3, 1), (2, 4), (1, 6), (2, 5), (2, 6), (3, 2), (1, 7), (3, 3), (2, 7), (4, 0), (4, 1),
    (3, 4), (3, 5), (3, 6), (4, 2), (4, 3), (3, 7), (5, 0), (5, 1), (4, 4), (4, 5), (4, 6), (5, 3), (5, 2), (4, 7), (6, 0),
    (6, 1), (5, 4), (5, 6), (5, 5), (5, 7), (6, 2), (6, 3), (6, 5), (11, 0), (12, 0), (6, 4), (6, 7), (6, 6), (11, 1), (12, 1),
    (11, 2), (12, 2), (13, 0), (11, 3), (12, 3), (13, 1), (11, 5), (12, 5), (13, 2), (11, 4), (12, 4), (11, 7), (13, 3),
    (12, 7), (13, 5), (11, 6), (12, 6), (13, 4), (13, 7), (13, 6), (14, 1), (15, 1), (14, 0), (15, 0), (16, 1), (14, 2),
    (16, 0), (15, 2), (14, 3), (19, 1), (15, 3), (14, 5), (19, 0), (16, 2), (14, 7), (15, 5), (15, 7), (14, 4), (20, 1),
    (15, 4), (16, 3), (20, 0), (14, 6), (19, 2), (15, 6), (16, 5), (16, 7), (21, 1), (16, 4), (19, 3), (21, 0), (20, 2),
    (16, 6), (19, 5), (22, 1), (19, 7), (20, 3), (19, 4), (22, 0), (21, 2), (19, 6), (23, 1), (20, 5), (20, 7), (24, 1),
    (20, 4), (21, 3), (23, 0), (26, 0), (26, 1), (22, 2), (24, 0), (20, 6), (21, 5), (21, 7), (21, 4), (22, 3), (25, 1),
    (21, 6), (23, 2), (22, 5), (26, 2), (22, 7), (22, 4), (25, 0), (24, 2), (23, 3), (26, 3), (22, 6), (24, 3), (23, 5),
    (23, 7), (23, 4), (24, 5), (24, 7), (26, 4), (26, 5), (23, 6), (24, 4), (25, 2), (26, 6), (24, 6), (26, 7), (25, 3),
    (25, 5), (25, 4), (25, 7), (25, 6),
)
ORDER_SECOND = (
    (0, 1), (0, 0), (0, 2), (0, 3), (0, 4), (0, 5), (0, 6), (0, 7), (14, 0), (15, 0), (14, 1), (15, 1), (14, 2), (14, 4),
    (14, 3), (15, 2), (15, 3), (14, 5), (15, 4), (16, 0), (14, 7), (15, 5), (16, 1), (14, 6), (15, 6), (16, 2), (16, 3),
    (15, 7), (16, 4), (16, 6), (16, 5), (1, 0), (16, 7), (2, 0), (1, 1), (2, 1), (1, 2), (3, 0), (2, 2), (3, 1), (1, 3),
    (2, 3), (4, 0), (3, 2), (1, 5), (4, 1), (2, 5), (1, 4), (3, 3), (5, 0), (2, 4), (1, 7), (4, 2), (5, 1), (2, 7), (3, 5),
    (1, 6), (4, 3), (6, 0), (19, 0), (2, 6), (3, 4), (6, 1), (19, 1), (5, 2), (3, 7), (4, 5), (5, 3), (20, 0), (3, 6), (4, 4),
    (20, 1), (6, 2), (19, 2), (4, 7), (5, 5), (21, 0), (6, 3), (19, 3), (4, 6), (5, 4), (21, 1), (5, 7), (20, 2), (6, 5),
    (19, 5), (20, 3), (5, 6), (22, 0), (22, 1), (6, 4), (19, 4), (6, 7), (19, 7), (21, 2), (20, 5), (21, 3), (6, 6), (19, 6),
    (23, 1), (20, 4), (23, 0), (20, 7), (24, 1), (24, 0), (22, 2), (21, 5), (22, 3), (20, 6), (21, 4), (21, 7), (23, 2),
    (22, 5), (25, 1), (24, 2), (21, 6), (23, 3), (25, 0), (22, 4), (22, 7), (24, 3), (23, 5), (22, 6), (24, 5), (23, 4),
    (23, 7), (25, 2), (7, 0), (7, 1), (7, 2), (7, 3), (7, 4), (24, 7), (7, 5), (7, 7), (7, 6), (24, 4), (23, 6), (25, 3),
    (24, 6), (25, 5), (8, 0), (8, 1), (8, 2), (8, 4), (8, 3), (8, 5), (25, 7), (8, 6), (8, 7), (9, 0), (9, 1), (9, 2), (25, 4),
    (9, 4), (9, 3), (9, 5), (9, 6), (9, 7), (25, 6), (10, 1), (10, 0), (10, 2), (10, 4), (10, 7), (10, 5), (10, 3), (10, 6),
    (11, 1), (11, 2), (26, 2), (11, 0), (26, 0), (26, 1), (12, 0), (12, 1), (12, 2), (11, 3), (26, 3), (12, 3), (11, 4),
    (26, 4), (11, 5), (26, 5), (12, 4), (12, 5), (11, 6), (12, 6), (26, 6), (13, 4), (11, 7), (26, 7), (13, 0), (12, 7),
    (13, 1), (13, 2), (13, 3), (13, 5), (13, 6), (13, 7),
)


def dot_nt(a, b):
    return lax.dot_general(a, b, (((1,), (1,)), ((), ())), preferred_element_type=F32)


def dot_tn(a, b):
    return lax.dot_general(a, b, (((0,), (0,)), ((), ())), preferred_element_type=F32)


RING, PAIRS, DIRECT, SHORT = 0, 1, 2, 3
PARENT = ((0, 1, 2, 3), (0, 0, 2, 2), (0, 0, 0, 0), (0, 1, 2, 2))
ROUTES_FIRST = {
    "u": (RING,) * 8,
    "h": (DIRECT,) * 8,
    "v": (PAIRS,) * 8,
    "d": (RING,) * 8,
}
ROUTES_SECOND = {
    "u": (RING,) * 8,
    "h": (RING,) * 8,
    "v": (PAIRS,) * 8,
    "d": (RING,) * 8,
}


def hops(b):
    return (4, 3) if b % 2 == 0 else (3, 4)


def legs(kind, b, stage):
    pairs = []
    for way, count in enumerate(hops(b)):
        if kind == RING:
            some = [count + 1 - stage]
        elif kind == PAIRS:
            some = [(3, 4, 1), (2,)][stage - 1]
        elif kind == SHORT:
            some = [(4, 3), (2,), (1,)][stage - 1]
        else:
            some = (3, 4, 2, 1)
        pairs += [(way, s) for s in some if 1 <= s <= count]
    return pairs


def children(kind, count, s):
    return [later for later in range(s + 1, count + 1) if PARENT[kind][later - 1] == s]


def waited(kind, s):
    return (kind == RING and s <= 3) or (kind == PAIRS and s == 2) or (kind == SHORT and s <= 2)


def row_column(value, rows):
    high = value.astype(BF16).astype(F32)
    lane = lax.broadcasted_iota(jnp.int32, (rows, LANES), 1)
    return jnp.where(lane == 0, high, jnp.where(lane == 1, value - high, 0.0))


def kernel(
    sizes,
    feed, gate_hbm, up_hbm, down_hbm,
    out_ref, grad_ref, gg_ref, gu_ref, gd_ref,
    w_pair, w_down, x_all, g_all,
    part_u, send_u, recv_u, part_v, send_v, recv_v,
    act, scale_r, h_all, d_all,
    core_src, core_dst, slab_src, slab_dst, row_src, out_dst,
    acc_pair, acc_down, stage_pair, stage_down,
    w_sem, feed_s, feed_r, bcast_s, bcast_r, core_s, core_r,
    rsu_s, rsu_r, rsv_s, rsv_r, agh_s, agh_r, agd_s, agd_r,
    slab_s, slab_r, row_s, out_s, out_r,
):
    nb, dp, chips, rows, width, hid, tokens = sizes
    half = width // 2
    batch = chips * rows
    chunk = batch // dp
    sec = lax.axis_index("section")
    d = lax.axis_index("dp")
    t = lax.axis_index("tensor")
    k = t // 2
    c = t % 2
    other = 1 - sec
    pair = 2 * hid

    def at(**axes):
        return axes

    def turn(base, step, size):
        return lax.rem(base + step + size, size)

    def z_at(step):
        return at(dp=turn(d, step, dp))

    def chip_at(j):
        return at(tensor=turn(k, j, chips) * 2 + c)

    sibling = at(tensor=k * 2 + (1 - c))

    def rcopy(src, dst, ss, rs, dev):
        return pltpu.make_async_remote_copy(
            src_ref=src, dst_ref=dst, send_sem=ss, recv_sem=rs, device_id=dev, device_id_type=MESH
        )

    loads = [
        pltpu.make_async_copy(gate_hbm, w_pair.at[pl.ds(0, hid)], w_sem.at[0]),
        pltpu.make_async_copy(up_hbm, w_pair.at[pl.ds(hid, hid)], w_sem.at[1]),
        pltpu.make_async_copy(down_hbm, w_down, w_sem.at[2]),
    ]
    for load in loads:
        load.start()
    stores = [
        pltpu.make_async_copy(stage_pair.at[pl.ds(0, hid)], gg_ref, w_sem.at[3]),
        pltpu.make_async_copy(stage_pair.at[pl.ds(hid, hid)], gu_ref, w_sem.at[4]),
        pltpu.make_async_copy(stage_down, gd_ref, w_sem.at[5]),
    ]

    barrier = pltpu.get_barrier_semaphore()
    for j in range(1, dp):
        pl.semaphore_signal(barrier, inc=1, device_id=z_at(j), device_id_type=MESH)
    for j in range(1, chips):
        pl.semaphore_signal(barrier, inc=1, device_id=chip_at(j), device_id_type=MESH)
    for j in range(chips):
        pl.semaphore_signal(
            barrier, inc=1, device_id=at(section=other, **chip_at(j)), device_id_type=MESH
        )
    for j in range(dp):
        pl.semaphore_signal(barrier, inc=1, device_id={**z_at(j), **sibling}, device_id_type=MESH)
    pl.semaphore_wait(barrier, dp - 1 + chips - 1 + chips + dp)

    ends = []

    def feed_all(into):
        for j in range(1, dp):
            rcopy(
                feed.at[turn(d, j, dp)], into.at[d, c, k], feed_s.at[0], feed_r.at[d], z_at(j)
            ).start()
        seven = feed.at[pl.ds(0, dp - 1)]
        ends.append(lambda: rcopy(seven, seven, feed_s.at[0], feed_r.at[0], z_at(1)).wait_send())
        into[d, c, k] = feed[d]

    def feed_slab(way, into, b):
        @pl.when(d != b)
        def _():
            rcopy(into.at[b, c, k], into.at[b, c, k], feed_s.at[0], feed_r.at[b], z_at(1)).wait_recv()

        for j in range(1, chips):
            rcopy(
                into.at[b, c, k], into.at[b, c, k], bcast_s.at[way, b], bcast_r.at[way, b], chip_at(j)
            ).start()
        seven = into.at[b, c, pl.ds(0, chips - 1)]
        ends.append(lambda: rcopy(seven, seven, bcast_s.at[way, b], bcast_r.at[way, b], z_at(1)).wait_send())

    def slabs_to_core(way, into, count, b):
        some = into.at[b, c, pl.ds(0, count)]
        rcopy(some, some, bcast_s.at[way, b], bcast_r.at[way, b], z_at(1)).wait_recv()
        own = into.at[b, c]
        copy = rcopy(own, own, core_s.at[way, b], core_r.at[way, b], sibling)
        copy.start()
        ends.append(copy.wait_send)

    def wait_core(way, into, b):
        rest = into.at[b, 1 - c]
        rcopy(rest, rest, core_s.at[way, b], core_r.at[way, b], sibling).wait_recv()

    def rs_copy(kind, way, s, src, dst, ss, rs, b):
        hop = (1 - 2 * way) * (s - PARENT[kind][s - 1])
        at_leg = (b, way, s - 1)
        return rcopy(src.at[at_leg], dst.at[at_leg], ss.at[at_leg], rs.at[at_leg], z_at(hop))

    def rs_step(stage, which, part, src, dst, ss, rs, b):
        kind = which[b]
        for way, s in legs(kind, b, stage):
            value = part[b, turn(d, (1 - 2 * way) * s, dp)]
            for later in children(kind, hops(b)[way], s):
                rs_copy(kind, way, later, src, dst, ss, rs, b).wait_recv()
                value = value + dst[b, way, later - 1].astype(F32)
            src[b, way, s - 1] = value.astype(BF16)
            copy = rs_copy(kind, way, s, src, dst, ss, rs, b)
            copy.start()
            ends.append(copy.wait_send)

    def rs_total(which, part, src, dst, ss, rs, b):
        kind = which[b]
        total = part[b, d]
        for way, count in enumerate(hops(b)):
            for s in children(kind, count, 0):
                rs_copy(kind, way, s, src, dst, ss, rs, b).wait_recv()
                total = total + dst[b, way, s - 1].astype(F32)
        return total

    def ag_copy(kind, way, s, buf, ss, rs, b, held):
        sign = 1 - 2 * way
        piece = buf.at[b, turn(d, -sign * held, dp)]
        return rcopy(
            piece, piece, ss.at[b, way, s - 1], rs.at[b, way, s - 1], z_at(sign * (s - PARENT[kind][s - 1]))
        )

    def ag_step(stage, which, buf, ss, rs, b):
        kind = which[b]
        held = 2 if kind == PAIRS and stage == 2 else stage - 1
        order = (3, 4, 2, 1) if held == 0 else (4, 3, 2, 1)
        for way, count in enumerate(hops(b)):
            if held:
                ag_copy(kind, way, held, buf, ss, rs, b, held).wait_recv()
            later = children(kind, count, held)
            for s in order:
                if s in later:
                    copy = ag_copy(kind, way, s, buf, ss, rs, b, held)
                    copy.start()
                    ends.append(copy.wait_send)

    def ag_finish(which, buf, ss, rs, b):
        kind = which[b]
        for way, count in enumerate(hops(b)):
            for s in range(1, count + 1):
                if not waited(kind, s):
                    ag_copy(kind, way, s, buf, ss, rs, b, s).wait_recv()

    routes = {}

    def rs_u():
        return (routes["u"], part_u, send_u, recv_u, rsu_s, rsu_r)

    def rs_v():
        return (routes["v"], part_v, send_v, recv_v, rsv_s, rsv_r)

    def ag_h():
        return (routes["h"], h_all, agh_s, agh_r)

    def ag_d():
        return (routes["d"], d_all, agd_s, agd_r)

    def whole(ref, b, count=1):
        parts = [ref[b : b + count, i].reshape(count * batch, half) for i in range(2)]
        return jnp.concatenate(parts, axis=1)

    def project_up(b):
        wait_core(0, x_all, b)
        x = whole(x_all, b)
        u = dot_nt(x, w_pair[...])
        xf = x.astype(F32)
        squares = jnp.sum(xf * xf, axis=1, keepdims=True)
        part_u[b, :, :, 0:pair] = u.reshape(dp, chunk, pair)
        part_u[b, :, :, pair:] = row_column(squares, batch).reshape(dp, chunk, LANES)
        rs_step(1, *rs_u(), b)

    def project_dh(b):
        wait_core(1, g_all, b)
        g = whole(g_all, b)
        part_v[b] = dot_nt(g, w_down[...]).reshape(dp, chunk, hid)
        rs_step(1, *rs_v(), b)

    def hidden(send, b):
        total = rs_total(*rs_u(), b)
        squares = jnp.sum(total[:, pair:], axis=1, keepdims=True)
        r = lax.rsqrt(squares / (width * dp) + EPS)
        ab = total[:, :pair] * r
        a, up = ab[:, :hid], ab[:, hid:]
        act[b] = ab
        scale_r[b] = jnp.broadcast_to(r, (chunk, LANES))
        h_all[b, d] = (a * jax.nn.sigmoid(a) * up).astype(BF16)
        if send:
            ag_step(1, *ag_h(), b)

    def hidden_grad(b):
        dh = rs_total(*rs_v(), b)
        r = scale_r[b][:, 0:1]
        a, up = act[b, :, :hid], act[b, :, hid:]
        sig = jax.nn.sigmoid(a)
        da = (r * (dh * up * sig * (1.0 + a * (1.0 - sig)))).astype(BF16)
        db = (r * (dh * a * sig)).astype(BF16)
        mixed = r * jnp.sum(da.astype(F32) * a + db.astype(F32) * up, axis=1, keepdims=True)
        d_all[b, d, :, 0:hid] = da
        d_all[b, d, :, hid:pair] = db
        d_all[b, d, :, pair:] = row_column(mixed, chunk).astype(BF16)
        ag_step(1, *ag_d(), b)

    def to_sibling(way, b):
        rest = core_src.at[way, b, 1 - c]
        copy = rcopy(rest, core_dst.at[way, b], core_s.at[2 + way, b], core_r.at[2 + way, b], sibling)
        copy.start()
        ends.append(copy.wait_send)

    def halves_out(way, value, b):
        for i in range(2):
            core_src[way, b, i] = value[:, i * half : (i + 1) * half].astype(BF16).reshape(chips, rows, half)

    def project_down(b):
        ag_finish(*ag_h(), b)
        h = h_all[b].reshape(batch, hid)
        p = jnp.dot(h, w_down[...], preferred_element_type=F32)
        halves_out(0, p, b)
        to_sibling(0, b)

    def project_dn(b):
        ag_finish(*ag_d(), b)
        flat = d_all[b].reshape(batch, pair + LANES)
        mixed = jnp.sum(flat[:, pair:].astype(F32), axis=1, keepdims=True)
        q = jnp.dot(flat[:, :pair], w_pair[...], preferred_element_type=F32)
        xf = whole(x_all, b).astype(F32)
        q = q - xf * (mixed * (1.0 / (width * dp)))
        halves_out(1, q, b)
        to_sibling(1, b)

    def scatter_slabs(way, b):
        rest = core_dst.at[way, b]
        rcopy(rest, rest, core_s.at[2 + way, b], core_r.at[2 + way, b], sibling).wait_recv()
        both = core_src[way, b, c].astype(F32) + core_dst[way, b].astype(F32)
        slab_src[way, b] = both.astype(BF16)
        for j in range(1, chips):
            to = turn(k, j, chips)
            rcopy(
                slab_src.at[way, b, to], slab_dst.at[way, b, k], slab_s.at[way, b], slab_r.at[way, b], chip_at(j)
            ).start()
        seven = slab_dst.at[way, b, pl.ds(0, chips - 1)]
        ends.append(lambda: rcopy(seven, seven, slab_s.at[way, b], slab_r.at[way, b], z_at(1)).wait_send())

    def slab_total(way, b):
        seven = slab_dst.at[way, b, pl.ds(0, chips - 1)]
        rcopy(seven, seven, slab_s.at[way, b], slab_r.at[way, b], z_at(1)).wait_recv()
        total = slab_src[way, b, k].astype(F32)
        for j in range(1, chips):
            total = total + slab_dst[way, b, turn(k, j, chips)].astype(F32)
        return total

    def finish_slab(way, value, into, b):
        row_src[way, b] = value.astype(BF16)
        if into is not None:
            for j in range(chips):
                rcopy(
                    row_src.at[way, b], into.at[b, c, k], row_s.at[way, b], bcast_r.at[way, b],
                    at(section=other, **chip_at(j)),
                ).start()
            eight = into.at[b, c]
            ends.append(lambda: rcopy(eight, eight, row_s.at[way, b], bcast_r.at[way, b], z_at(1)).wait_send())
        source = d * 2 + c
        crossed = rcopy(
            row_src.at[way, b], out_dst.at[way, source], out_s.at[way, b, 1], out_r.at[way], {"dp": b, **sibling}
        )
        crossed.start()
        ends.append(crossed.wait_send)
        copy = rcopy(row_src.at[way, b], out_dst.at[way, source], out_s.at[way, b, 0], out_r.at[way], at(dp=b))

        @pl.when(d == b)
        def _():
            out_dst[way, source] = row_src[way, b]

        @pl.when(d != b)
        def _():
            copy.start()

        def end():
            @pl.when(d != b)
            def _():
                copy.wait_send()

        ends.append(end)

    def finish_out(into, b):
        finish_slab(0, x_all[b, c, k].astype(F32) + slab_total(0, b), into, b)

    def finish_grad(into, b):
        finish_slab(1, g_all[b, c, k].astype(F32) + slab_total(1, b), into, b)

    def weight_grads(b):
        if b % 2 == 0:
            return
        x = whole(x_all, b - 1, 2)
        g = whole(g_all, b - 1, 2)
        pair_part = dot_tn(d_all[b - 1 : b + 1].reshape(2 * batch, pair + LANES)[:, :pair], x)
        down_part = dot_tn(h_all[b - 1 : b + 1].reshape(2 * batch, hid), g)
        if b == 1:
            acc_pair[...] = pair_part
            acc_down[...] = down_part
        elif b < nb - 1:
            acc_pair[...] += pair_part
            acc_down[...] += down_part
        else:
            scale = 1.0 / math.sqrt(tokens)
            stage_pair[...] = ((acc_pair[...] + pair_part) * scale).astype(BF16)
            stage_down[...] = ((acc_down[...] + down_part) * scale).astype(BF16)
            for store in stores:
                store.start()

    def collect(way, ref):
        rest = out_dst.at[way, pl.ds(0, 2 * dp - 1)]
        rcopy(rest, rest, out_s.at[way, 0, 0], out_r.at[way], z_at(1)).wait_recv()
        for source in range(2 * dp):
            block = out_dst[way, source].astype(F32)
            ref[:, source * half : (source + 1) * half] = jnp.where(c == 0, block[: rows // 2], block[rows // 2 :])

    def part(function, *args):
        return functools.partial(function, *args)

    def wait_weights():
        for load in loads:
            load.wait()

    def close():
        collect(0, out_ref)
        collect(1, grad_ref)
        for end in ends:
            end()
        for store in stores:
            store.wait()
        ends.clear()

    def run(order, kinds, x_slabs, g_slabs, feed_op, hidden_op, out_op, grad_op):
        routes.update(kinds)
        ops = [
            feed_op,
            part(slabs_to_core, 0, x_all, x_slabs),
            project_up,
            *[part(rs_step, step, *rs_u()) for step in (2, 3, 4)],
            hidden_op,
            *[part(ag_step, step, *ag_h()) for step in (1, 2, 3, 4)],
            project_down,
            part(scatter_slabs, 0),
            out_op,
            part(slabs_to_core, 1, g_all, g_slabs),
            project_dh,
            *[part(rs_step, step, *rs_v()) for step in (2, 3, 4)],
            hidden_grad,
            *[part(ag_step, step, *ag_d()) for step in (2, 3, 4)],
            project_dn,
            part(scatter_slabs, 1),
            grad_op,
            weight_grads,
        ]
        for op, b in order:
            ops[op](b)

    @pl.when(sec == 0)
    def _():
        feed_all(x_all)
        wait_weights()
        run(
            ORDER_FIRST, ROUTES_FIRST, chips - 1, chips, part(feed_slab, 0, x_all), part(hidden, True),
            part(finish_out, x_all), part(finish_grad, None),
        )
        close()

    @pl.when(sec == 1)
    def _():
        feed_all(g_all)
        wait_weights()
        run(
            ORDER_SECOND, ROUTES_SECOND, chips, chips - 1, part(feed_slab, 1, g_all), part(hidden, False),
            part(finish_out, None), part(finish_grad, g_all),
        )
        close()


def finish_kernel(out_in, grad_in, gg_in, gu_in, gd_in, out_ref, grad_ref, gg_ref, gu_ref, gd_ref):
    share = out_ref.shape[2]
    for src, dst in ((out_in, out_ref), (grad_in, grad_ref)):
        for m in range(out_ref.shape[1]):
            dst[0, m] = src[m * share : (m + 1) * share].astype(BF16)
    for src, dst in ((gg_in, gg_ref), (gu_in, gu_ref), (gd_in, gd_ref)):
        dst[0] = src[...]


def shards(inputs, cotangent, gate_weight, up_weight, down_weight):
    first = lax.axis_index("section") == 0
    dp, tensors = lax.axis_size("dp"), lax.axis_size("tensor")
    micro, tok_dev, model = inputs.shape
    _, hid, width = gate_weight.shape
    chips = tensors // 2
    share = tok_dev // tensors
    held = micro * share
    nb, rows, half = dp, 2 * held, width // 2
    chunk = chips * rows // dp
    pair = 2 * hid
    tensor = lax.axis_index("tensor")
    start = tensor // 2 * (2 * share)
    pick = jnp.where(
        first,
        lax.dynamic_slice_in_dim(inputs, start, 2 * share, 1),
        lax.dynamic_slice_in_dim(cotangent, start, 2 * share, 1),
    )
    pick = pick.reshape(micro, 2, share, dp, 2, half)
    pick = jnp.where(tensor % 2 == 0, pick[:, :, :, :, 0], pick[:, :, :, :, 1])
    feed = pick.transpose(3, 1, 0, 2, 4).reshape(dp, rows, half)

    def sems(*shape):
        return pltpu.SemaphoreType.DMA(shape)

    def bf16(*shape):
        return pltpu.VMEM(shape, BF16)

    def f32(*shape):
        return pltpu.VMEM(shape, F32)

    sizes = (nb, dp, chips, rows, width, hid, micro * tok_dev * dp)
    vmem = pl.BlockSpec(memory_space=pltpu.VMEM)
    anywhere = pl.BlockSpec(memory_space=pl.ANY)
    out, grad, grad_gate, grad_up, grad_down = pl.pallas_call(
        functools.partial(kernel, sizes),
        out_shape=[
            jax.ShapeDtypeStruct((held, model), F32),
            jax.ShapeDtypeStruct((held, model), F32),
            jax.ShapeDtypeStruct((hid, width), BF16),
            jax.ShapeDtypeStruct((hid, width), BF16),
            jax.ShapeDtypeStruct((hid, width), BF16),
        ],
        in_specs=[vmem, anywhere, anywhere, anywhere],
        out_specs=[vmem, vmem, anywhere, anywhere, anywhere],
        scratch_shapes=[
            bf16(pair, width),
            bf16(hid, width),
            bf16(nb, 2, chips, rows, half),
            bf16(nb, 2, chips, rows, half),
            f32(nb, dp, chunk, pair + LANES),
            bf16(nb, 2, 4, chunk, pair + LANES),
            bf16(nb, 2, 4, chunk, pair + LANES),
            f32(nb, dp, chunk, hid),
            bf16(nb, 2, 4, chunk, hid),
            bf16(nb, 2, 4, chunk, hid),
            f32(nb, chunk, pair),
            f32(nb, chunk, LANES),
            bf16(nb, dp, chunk, hid),
            bf16(nb, dp, chunk, pair + LANES),
            bf16(2, nb, 2, chips, rows, half),
            bf16(2, nb, chips, rows, half),
            bf16(2, nb, chips, rows, half),
            bf16(2, nb, chips, rows, half),
            bf16(2, nb, rows, half),
            bf16(2, 2 * dp, rows, half),
            f32(pair, width),
            f32(hid, width),
            bf16(pair, width),
            bf16(hid, width),
            sems(6),
            sems(1),
            sems(dp),
            sems(2, nb),
            sems(2, nb),
            sems(4, nb),
            sems(4, nb),
            *[sems(nb, 2, 4) for _ in range(8)],
            sems(2, nb),
            sems(2, nb),
            sems(2, nb),
            sems(2, nb, 2),
            sems(2),
        ],
        compiler_params=pltpu.CompilerParams(
            collective_id=0, has_side_effects=True, vmem_limit_bytes=56 * 1024 * 1024
        ),
    )(feed, gate_weight[0], up_weight[0], down_weight[0])
    return pl.pallas_call(
        finish_kernel,
        out_shape=[
            jax.ShapeDtypeStruct((1, micro, share, model), BF16),
            jax.ShapeDtypeStruct((1, micro, share, model), BF16),
            jax.ShapeDtypeStruct((1, hid, width), BF16),
            jax.ShapeDtypeStruct((1, hid, width), BF16),
            jax.ShapeDtypeStruct((1, hid, width), BF16),
        ],
        in_specs=[vmem] * 5,
        out_specs=[vmem] * 5,
    )(out, grad, grad_gate, grad_up, grad_down)


def solution(mesh):
    in_specs = (
        P(None, "dp", None),
        P(None, "dp", None),
        P("section", "tensor", "dp"),
        P("section", "tensor", "dp"),
        P("section", "tensor", "dp"),
    )
    out_specs = (
        P("section", None, ("dp", "tensor"), None),
        P("section", None, ("dp", "tensor"), None),
        P("section", "tensor", "dp"),
        P("section", "tensor", "dp"),
        P("section", "tensor", "dp"),
    )
    return jax.shard_map(shards, mesh=mesh, in_specs=in_specs, out_specs=out_specs, check_vma=False)
```
